768 devices in a mesh: rep: 4 (over z_hi, core), occ: 6 (over z_lo), vir: 32 (over x, y).
Axes of the slice: x: 4, y: 8, z: 12 (z_hi: 2, z_lo: 6; z = z_hi * 6 + z_lo), core: 2. Of those that a mesh axis runs over, the one named last changes fastest.
Arguments:
- amplitudes: bfloat16 [3072, 12288], P('occ', ('rep', 'vir')), may hold values from -6 to 6
- ladder_ints: bfloat16 [12288, 12288], P('rep', 'vir'), may hold values from -0.15625 to 0.15625
- cycle_ints: bfloat16 [3072, 3072], P('occ'), may hold values from -0.3125 to 0.3125
- occ_irrep: int32 [3072], replicated, may hold values from 0 to 7
- vir_irrep: int32 [12288], replicated, may hold values from 0 to 7
Outputs:
- residual_update: bfloat16 [3072, 12288], P('occ', 'vir')
The draws below stay inside these ranges and needn't reach their ends.
Inputs may be any that keep to these rules, and one draw needn't show every extreme that they name: `occ_irrep`: irrep labels of the point group. `vir_irrep`: irrep labels of the point group; the sectors are of unequal sizes.
All inputs are finite; a program needn't handle non-finite values.
Results may differ from the reference program's by a relative error of at most 0.004.
Values may be sent and summed in bfloat16 or wider, within the bound.
A program may use at most 32 MiB of HBM per device.

```python
import math
import jax
import jax.numpy as jnp
import numpy as np

NPAIR = 3072
NVP = 12288


def plant(entries, rng, least, high):
    longest = entries.shape.index(max(entries.shape))
    spots = []
    for shift in (0, 1):
        where = [jax.random.randint(jax.random.fold_in(rng, axis), (), 0, length) for axis, length in enumerate(entries.shape)]
        where[longest] = (where[longest] + shift) % entries.shape[longest]
        spots.append(tuple(where))
    return entries.at[spots[0]].set(least).at[spots[1]].set(high)


def shard_levels(key, shape, split, smallest, top_value):
    level = 1.0
    for axis_at, parts in split:
        draws = jax.random.uniform(jax.random.fold_in(jax.random.fold_in(key, 6), axis_at), (parts,), jnp.float32, smallest / len(split), top_value / len(split))
        level = level * jnp.repeat(jnp.exp(draws), shape[axis_at] // parts).reshape((-1,) + (1,) * (len(shape) - 1 - axis_at))
    return level


def cumulative_ranks(count, skew):
    loads = [(1 << 20) // math.isqrt(standing ** skew) + 1 for standing in range(1, count + 1)]
    scale = 1 + sum(loads) // (1 << 30)
    return np.cumsum(np.array([max(1, weight // scale) for weight in loads]))


def skewed_ids(own_key, dims, count, skew):
    listing = cumulative_ranks(count, skew)
    pick = jax.random.randint(jax.random.fold_in(own_key, 1), dims, 0, int(listing[count - 1]))
    rank = jnp.searchsorted(jnp.asarray(listing, jnp.int32), pick, side="right")
    return jax.random.permutation(jax.random.fold_in(own_key, 2), count)[rank].astype(jnp.int32)


def bell_draw(stream_key, extent, spread, reach, split=(), held_as=jnp.bfloat16):
    array = spread * jax.random.normal(stream_key, extent, jnp.float32)
    if split:
        array = array * shard_levels(stream_key, extent, split, -0.22, 0.18)
    return jnp.clip(array, -reach, reach).astype(held_as)


def setup_inputs(seed: int = 0) -> dict:
    keys = jax.random.split(jax.random.key(seed), 6)
    amplitudes = bell_draw(keys[0], (NPAIR, NVP), 1.0, 6.0, ((0, 6), (1, 128)))
    ladder_ints = bell_draw(keys[1], (NVP, NVP), (NVP // 8) ** -0.5, 0.15625, ((0, 4), (1, 32)))
    cycle_ints = bell_draw(keys[2], (NPAIR, NPAIR), (NPAIR // 8) ** -0.5, 0.3125, ((0, 6),))
    occ_irrep = plant(jax.random.randint(keys[3], (NPAIR,), 0, 8), jax.random.fold_in(keys[3], 1), 0, 7).astype(jnp.int32)
    vir_irrep = plant(skewed_ids(keys[4], (NVP,), 8, 1), jax.random.fold_in(keys[4], 3), 0, 7).astype(jnp.int32)
    return dict(amplitudes=amplitudes, ladder_ints=ladder_ints, cycle_ints=cycle_ints, occ_irrep=occ_irrep, vir_irrep=vir_irrep)


def reference(amplitudes, ladder_ints, cycle_ints, occ_irrep, vir_irrep):
    zero = jnp.zeros((), jnp.bfloat16)
    sector_amps = jnp.where(occ_irrep[:, None] == vir_irrep[None, :], amplitudes, zero)
    sector_ladder = jnp.where(vir_irrep[:, None] == vir_irrep[None, :], ladder_ints, zero)
    ladder = jnp.dot(sector_amps, sector_ladder, preferred_element_type=jnp.float32)
    ladder_b = ladder.astype(jnp.bfloat16)
    sector_cycle = jnp.where(occ_irrep[:, None] == occ_irrep[None, :], cycle_ints, zero)
    cycle = jnp.dot(sector_cycle, ladder_b, preferred_element_type=jnp.float32)
    return (ladder + cycle).astype(jnp.bfloat16)
```

```python
import functools

import jax
import jax.numpy as jnp
from jax import lax
from jax.experimental import pallas as pl
from jax.experimental.pallas import tpu as pltpu
from jax.sharding import PartitionSpec as P

MESH = pl.DeviceIdType.MESH
BF, F32 = jnp.bfloat16, jnp.float32
NX, NY, NZ = 4, 8, 12
GROUPS, ROWS, CAP, LANES = 6, 512, 96, 128
OWN, COLS, DEPTH = 96, 384, 3072
HALF = CAP // 2
MAIN, SPARE = 80, LANES - CAP
Y_ORDER = (0, 1, 2, 3, 7, 6, 5, 4)
LAST_Y = Y_ORDER[-1]
Z_STEPS = (1, 2, 3, 9, 10, 11)
TOP = 32000.0


def onehot(labels):
    width = labels.shape[1]
    rows = lax.broadcasted_iota(jnp.int32, (16, width), 0)
    return jnp.where(jnp.broadcast_to(labels, (16, width)) == rows, 1.0, 0.0).astype(BF)


def meet(a, b):
    return lax.dot_general(a, b, (((0,), (0,)), ((), ())), preferred_element_type=F32)


def kernel(
    amps_in, lad_ref, cyc_ref, occ_in, vir_in, out_ref, flag_ref,
    amps_ref, occ_ref, vir_ref, lad, cyc, cbuf, racc, rin, pbuf, psc, qbuf, sbuf, ucat, lcat, omask,
    load_sem, y_send, x_send, c_recv, r_send, r_recv, q_send, s_send, q_recv, s_recv,
    g_send, gs_send, g_recv, gs_recv, f_send, fs_send, ready_x, ready_y, ready_z,
):
    rep, occ, vir = lax.axis_index("rep"), lax.axis_index("occ"), lax.axis_index("vir")
    x, y, z, core = vir // NY, vir % NY, (rep // 2) * GROUPS + occ, rep % 2

    def at(x1, y1, z1, core1):
        return {"rep": (z1 // GROUPS) * 2 + core1, "occ": z1 % GROUPS, "vir": x1 * NY + y1}

    def turn_x(x1):
        return jnp.where(x1 < 2, x1, 5 - x1)

    def turn_y(y1):
        return jnp.where(y1 < 4, y1, 11 - y1)

    def copy(src, dst, send, recv, where):
        return pltpu.make_async_remote_copy(
            src_ref=src, dst_ref=dst, send_sem=send, recv_sem=recv, device_id=where, device_id_type=MESH
        )

    loads = [
        pltpu.make_async_copy(a, b, load_sem.at[i])
        for i, (a, b) in enumerate(((occ_in, occ_ref), (vir_in, vir_ref), (amps_in, amps_ref)), 2)
    ]
    for load in loads:
        load.start()
    load_lad = pltpu.make_async_copy(lad_ref, lad, load_sem.at[0])
    load_cyc = pltpu.make_async_copy(cyc_ref, cyc, load_sem.at[1])
    load_lad.start()
    load_cyc.start()

    contacts = [((x, y1, z, core), ready_y.at[y], turn_y(y1) > turn_y(y), y1 != y) for y1 in range(NY)]
    contacts += [((x1, y, z, core), ready_x.at[x], turn_x(x1) > turn_x(x), x1 != x) for x1 in range(NX)]
    contacts += [
        ((x, y, (z + d) % NZ, core), ready_z.at[NZ - d], (z + d) % NZ > z, core < 2) for d in Z_STEPS
    ]
    barrier = pltpu.get_barrier_semaphore()
    sibling = at(x, y, z, 1 - core)
    pl.semaphore_signal(barrier, inc=1, device_id=sibling, device_id_type=MESH)
    for where, _, later, other in contacts:
        @pl.when(later & other)
        def _(where=where):
            pl.semaphore_signal(barrier, inc=1, device_id=at(*where), device_id_type=MESH)

    lower = sum(((z + d) % NZ < z).astype(jnp.int32) for d in Z_STEPS)
    pl.semaphore_wait(barrier, turn_x(x) + turn_y(y) + lower + 1)
    for where, ready, later, other in contacts:
        @pl.when(jnp.logical_not(later) & other)
        def _(where=where, ready=ready):
            pl.semaphore_signal(ready, inc=1, device_id=at(*where), device_id_type=MESH)

    for load in loads:
        load.wait()

    upper = lax.broadcasted_iota(jnp.int32, (ROWS, ROWS), 0) < lax.broadcasted_iota(jnp.int32, (ROWS, ROWS), 1)
    upper = jnp.where(upper, 1.0, 0.0).astype(BF)
    slot_ids = lax.broadcasted_iota(jnp.int32, (LANES, ROWS), 0).astype(F32)

    def slot_matrix(hot):
        before = jnp.dot(hot, upper, preferred_element_type=F32)
        rank = jnp.sum(before * hot.astype(F32), axis=0, keepdims=True)
        return jnp.where(jnp.broadcast_to(rank, (LANES, ROWS)) == slot_ids, 1.0, 0.0)

    occ_hot = onehot(occ_ref[:, pl.ds(pl.multiple_of(occ * ROWS, ROWS), ROWS)])
    own_slots = slot_matrix(occ_hot)
    first = (rep * 32 + vir) * OWN
    base = pl.multiple_of(jnp.minimum(first // 128, 94) * 128, 128)
    window = jnp.broadcast_to(vir_ref[:, pl.ds(base, 256)], (8, 256))
    window = pltpu.roll(window, (256 - (first - base)) % 256, 1)
    own_hot = onehot(window[0:1, :128])
    mask = meet(own_hot, occ_hot)[:OWN, :]
    sector = jnp.where(mask > 0.5, amps_ref[...].astype(F32), 0.0).astype(BF)

    def place(columns, slots):
        return lax.dot_general(
            columns, slots.astype(BF), (((1,), (1,)), ((), ())), preferred_element_type=F32
        )

    no_slots = jnp.zeros((SPARE, ROWS), F32)
    chunk = place(sector[:MAIN], jnp.concatenate([own_slots[:CAP], no_slots], axis=0))
    aside = [
        place(sector[MAIN:], jnp.concatenate([no_slots] * 3 + [own_slots[j * SPARE:(j + 1) * SPARE]], axis=0))
        for j in range(3)
    ]
    aside.append(jnp.zeros((MAIN - 3 * (OWN - MAIN), LANES), F32))
    cbuf[vir] = (chunk + jnp.concatenate(aside, axis=0)).astype(BF)

    def y_copy(y1):
        return copy(cbuf.at[vir], cbuf.at[vir], y_send.at[y1], c_recv.at[vir], at(x, y1, z, core))

    def x_copy(y1, d):
        v = x * NY + y1
        return copy(cbuf.at[v], cbuf.at[v], x_send.at[y1, d], c_recv.at[v], at((x + d) % NX, y, z, core))

    def c_wait(v):
        copy(cbuf.at[v], cbuf.at[v], y_send.at[0], c_recv.at[v], at(x, (y + 1) % NY, z, core)).wait_recv()

    def relay(y1):
        for d in (2, 1, 3):
            x_copy(y1, d).start()

    for y1 in Y_ORDER:
        @pl.when(turn_y(y1) < turn_y(y))
        def _(y1=y1):
            y_copy(y1).start()
    for x1 in range(NX):
        @pl.when(turn_x(x1) > turn_x(x))
        def _(x1=x1):
            pl.semaphore_wait(ready_x.at[x1], 1)
    relay(y)

    col_hot = onehot(vir_ref[:, pl.ds(pl.multiple_of(vir * COLS, 128), COLS)])

    def mask_ladder(i):
        blocks = slice(4 * i, 4 * i + 4)
        row_hot = onehot(vir_ref[:, pl.ds(pl.multiple_of(rep * DEPTH + i * COLS, 128), COLS)])
        keep = meet(row_hot, col_hot)
        rows = lad[blocks].reshape(COLS, COLS).astype(F32)
        lad[blocks] = jnp.where(keep > 0.5, rows, 0.0).astype(BF).reshape(4, OWN, COLS)

    def pack_cycle(g):
        hot = onehot(occ_ref[:, g * ROWS:(g + 1) * ROWS])
        most = jnp.max(jnp.sum(hot.astype(F32), axis=1, keepdims=True))
        group_slots = slot_matrix(hot).astype(BF)
        keep = meet(occ_hot, hot)
        part = jnp.where(keep > 0.5, cyc[:, g * ROWS:(g + 1) * ROWS].astype(F32), 0.0).astype(BF)
        moved = lax.dot_general(part, group_slots, (((1,), (1,)), ((), ())), preferred_element_type=F32)
        ucat[:, g * LANES:(g + 1) * LANES] = moved.astype(BF)
        return most

    def prepare():
        load_lad.wait()
        for i in range(8):
            mask_ladder(i)
        load_cyc.wait()
        worst = jnp.zeros((), F32)
        for g in range(GROUPS):
            worst = jnp.maximum(worst, pack_cycle(g))
        flag_ref[0] = jnp.where(worst > CAP, 1, 0)
        plain = own_slots.T.astype(BF)
        ucat[:, 6 * LANES:7 * LANES] = plain
        ucat[:, 7 * LANES:8 * LANES] = plain
        omask[...] = meet(occ_hot, col_hot)
        lcat[...] = jnp.zeros_like(lcat)

    early = turn_y(y) < 3
    pl.when(early)(prepare)
    for y1 in Y_ORDER:
        @pl.when(turn_y(y1) > turn_y(y))
        def _(y1=y1):
            pl.semaphore_wait(ready_y.at[y1], 1)
            y_copy(y1).start()
    for d in (1, 7, 2, 6, 3, 5, 4):
        source = lax.rem(y + d, NY)

        @pl.when(source != LAST_Y)
        def _(source=source):
            c_wait(x * NY + source)
            relay(source)

    @pl.when(y != LAST_Y)
    def _():
        c_wait(x * NY + LAST_Y)
        relay(LAST_Y)
    pl.when(jnp.logical_not(early))(prepare)

    def product(start):
        block, rows = cbuf[start:start + NY], lad[start:start + NY]

        def dot(a, b):
            a, b = a.reshape(-1, LANES), b.reshape(-1, COLS)
            return lax.dot_general(a, b, (((0,), (0,)), ((), ())), preferred_element_type=F32)

        main = dot(block[:, :MAIN], rows[:, :MAIN])[:CAP]
        step = OWN - MAIN
        aside = [dot(block[:, j * step:(j + 1) * step], rows[:, MAIN:])[CAP:] for j in range(3)]
        return main + jnp.concatenate(aside, axis=0)

    for x1 in range(NX):
        @pl.when(x1 != x)
        def _(x1=x1):
            for y1 in range(NY):
                c_wait(x1 * NY + y1)
    racc[...] = product(0)
    for x1 in range(1, NX):
        racc[...] += product(x1 * NY)

    mine = pl.ds(pl.multiple_of(core * HALF, HALF), HALF)
    theirs = pl.ds(pl.multiple_of((1 - core) * HALF, HALF), HALF)
    half_copy = copy(racc.at[theirs], rin, r_send, r_recv, sibling)
    half_copy.start()
    half_copy.wait_recv()
    total = racc[mine, :] + rin[...]

    def pack(values, into, scale):
        largest = jnp.max(jnp.max(jnp.abs(values), axis=1, keepdims=True), axis=0, keepdims=True)
        largest = jnp.maximum(largest, 1e-30)
        into[...] = jnp.round(values * (TOP / largest)).astype(jnp.int32).astype(jnp.int16)
        scale[...] = jnp.broadcast_to(largest * (1.0 / TOP), (8, 128))

    def unpack(packed, scale):
        return packed[...].astype(jnp.int32).astype(F32) * scale[0:1, 0:1]

    def send(q, s, to_q, to_s, sems, where):
        return copy(q, to_q, sems[0], sems[1], where), copy(s, to_s, sems[2], sems[3], where)

    def part_copy(i):
        d = (3, 9)[i]
        sems = q_send.at[i], q_recv.at[i], s_send.at[i], s_recv.at[i]
        return send(pbuf.at[2], psc.at[2], pbuf.at[i], psc.at[i], sems, at(x, y, (z + d) % NZ, core))

    group = lax.rem(z + 3, GROUPS)

    def group_copy(d):
        sems = g_send.at[d % NZ], g_recv.at[group, core], gs_send.at[d % NZ], gs_recv.at[group, core]
        to = qbuf.at[group, mine], sbuf.at[group, core]
        return send(*to, *to, sems, at(x, y, (z + d + NZ) % NZ, core))

    def side_copy(g):
        sems = f_send.at[g], g_recv.at[g, core], fs_send.at[g], gs_recv.at[g, core]
        to = qbuf.at[g, mine], sbuf.at[g, core]
        return send(*to, *to, sems, sibling)

    def group_wait(g, half):
        rows = pl.ds(pl.multiple_of(half * HALF, HALF), HALF)
        to = qbuf.at[g, rows], sbuf.at[g, half]
        sems = f_send.at[0], g_recv.at[g, half], fs_send.at[0], gs_recv.at[g, half]
        for c in send(*to, *to, sems, sibling):
            c.wait_recv()

    pack(total, pbuf.at[2], psc.at[2])
    for d in Z_STEPS:
        @pl.when((z + d) % NZ > z)
        def _(d=d):
            pl.semaphore_wait(ready_z.at[d], 1)
    for i in range(2):
        for c in part_copy(i):
            c.start()
    for i in range(2):
        for c in part_copy(i):
            c.wait_recv()
    both = unpack(pbuf.at[0], psc.at[0]) + unpack(pbuf.at[1], psc.at[1])
    pack(both, qbuf.at[group, mine], sbuf.at[group, core])
    far = jnp.where(core == 0, 3, 9)
    far_copy = [
        copy(a, a, sems[0], sems[1], at(x, y, lax.rem(z + far, NZ), core))
        for a, sems in (
            (qbuf.at[group, mine], (g_send.at[3], g_recv.at[group, core])),
            (sbuf.at[group, core], (gs_send.at[3], gs_recv.at[group, core])),
        )
    ]
    for c in far_copy:
        c.start()
    for d in (2, -2, 1, -1):
        for c in group_copy(d):
            c.start()
    for c in side_copy(group):
        c.start()
    for d in (1, -1, 2, -2, 3):
        g = lax.rem(z - d + 3 + NZ, GROUPS)
        group_wait(g, core)
        for c in side_copy(g):
            c.start()

    def whole(g):
        scale = jnp.concatenate(
            [jnp.broadcast_to(sbuf[g, h][0:1, 0:1], (HALF, COLS)) for h in range(2)], axis=0
        )
        return qbuf[g].astype(jnp.int32).astype(F32) * scale

    for g in range(GROUPS):
        group_wait(g, 1 - core)
        lcat[g * LANES:g * LANES + CAP, :] = whole(g).astype(BF)
    own = whole(occ)
    high = own.astype(BF)
    lcat[6 * LANES:6 * LANES + CAP, :] = high
    lcat[7 * LANES:7 * LANES + CAP, :] = (own - high.astype(F32)).astype(BF)
    result = jnp.dot(ucat[...], lcat[...], preferred_element_type=F32)
    out_ref[...] = jnp.where(omask[...] > 0.5, result, 0.0).astype(BF)

    for y1 in range(NY):
        @pl.when(y1 != y)
        def _(y1=y1):
            y_copy(y1).wait_send()
        for d in range(1, NX):
            x_copy(y1, d).wait_send()
    half_copy.wait_send()
    for i in range(2):
        for c in part_copy(i):
            c.wait_send()
    for c in far_copy:
        c.wait_send()
    for d in (2, -2, 1, -1):
        for c in group_copy(d):
            c.wait_send()
    for g in range(GROUPS):
        for c in side_copy(g):
            c.wait_send()


def compact(amplitudes, ladder_ints, cycle_ints, occ_irrep, vir_irrep):
    vmem, dma = pltpu.VMEM, pltpu.SemaphoreType.DMA
    return pl.pallas_call(
        kernel,
        out_shape=(jax.ShapeDtypeStruct((ROWS, COLS), BF), jax.ShapeDtypeStruct((1,), jnp.int32)),
        in_specs=[pl.BlockSpec(memory_space=pl.ANY)] * 5,
        out_specs=(pl.BlockSpec(memory_space=vmem), pl.BlockSpec(memory_space=pltpu.SMEM)),
        scratch_shapes=[
            vmem((OWN, ROWS), BF),
            vmem((1, GROUPS * ROWS), jnp.int32),
            vmem((1, NX * NY * COLS), jnp.int32),
            vmem((NX * NY, OWN, COLS), BF),
            vmem((ROWS, GROUPS * ROWS), BF),
            vmem((NX * NY, MAIN, LANES), BF),
            vmem((CAP, COLS), F32),
            vmem((HALF, COLS), F32),
            vmem((3, HALF, COLS), jnp.int16),
            vmem((3, 8, 128), F32),
            vmem((GROUPS, CAP, COLS), jnp.int16),
            vmem((GROUPS, 2, 8, 128), F32),
            vmem((ROWS, 8 * LANES), BF),
            vmem((8 * LANES, COLS), BF),
            vmem((ROWS, COLS), F32),
            dma((5,)),
            dma((NY,)),
            dma((NY, NX)),
            dma((NX * NY,)),
            dma,
            dma,
            dma((2,)),
            dma((2,)),
            dma((2,)),
            dma((2,)),
            dma((NZ,)),
            dma((NZ,)),
            dma((GROUPS, 2)),
            dma((GROUPS, 2)),
            dma((GROUPS,)),
            dma((GROUPS,)),
            pltpu.SemaphoreType.REGULAR((NX,)),
            pltpu.SemaphoreType.REGULAR((NY,)),
            pltpu.SemaphoreType.REGULAR((NZ,)),
        ],
        compiler_params=pltpu.CompilerParams(
            collective_id=0, has_side_effects=True, vmem_limit_bytes=48 * 1024 * 1024
        ),
        cost_estimate=pl.CostEstimate(flops=2_000_000_000, bytes_accessed=6_500_000, transcendentals=0),
    )(amplitudes.T, ladder_ints.reshape(NX * NY, OWN, COLS), cycle_ints, occ_irrep.reshape(1, -1), vir_irrep.reshape(1, -1))


def ring(axis, block, n):
    me = lax.axis_index(axis)
    perm = [(i, (i + 1) % n) for i in range(n)]
    held = jnp.zeros((n,) + block.shape, block.dtype)

    def step(s, carry):
        held, block = carry
        held = lax.dynamic_update_index_in_dim(held, block, (me - s + n) % n, 0)
        return held, lax.ppermute(block, axis, perm)

    held, _ = lax.fori_loop(0, n, step, (held, block))
    return held


def dense(amplitudes, ladder_ints, cycle_ints, occ_irrep, vir_irrep):
    rep_pos, vir_pos, occ_pos = lax.axis_index("rep"), lax.axis_index("vir"), lax.axis_index("occ")
    zero = jnp.zeros((), BF)
    occ_own = lax.dynamic_slice_in_dim(occ_irrep, occ_pos * ROWS, ROWS)
    own_labels = lax.dynamic_slice_in_dim(vir_irrep, (rep_pos * 32 + vir_pos) * OWN, OWN)
    sector_amps = jnp.where(occ_own[:, None] == own_labels[None, :], amplitudes, zero)
    group_labels = lax.dynamic_slice_in_dim(vir_irrep, rep_pos * DEPTH, DEPTH)
    column_labels = lax.dynamic_slice_in_dim(vir_irrep, vir_pos * COLS, COLS)
    sector_ladder = jnp.where(group_labels[:, None] == column_labels[None, :], ladder_ints, zero)
    sector_cycle = jnp.where(occ_own[:, None] == occ_irrep[None, :], cycle_ints, zero)
    gathered = ring("vir", sector_amps, NX * NY).transpose(1, 0, 2).reshape(ROWS, DEPTH)
    partial_ladder = jnp.dot(gathered, sector_ladder, preferred_element_type=F32)
    parts = ring("rep", partial_ladder, 4)
    ladder = (parts[0] + parts[1]) + (parts[2] + parts[3])
    ladder_all = ring("occ", ladder.astype(BF), GROUPS).reshape(GROUPS * ROWS, COLS)
    cycle = jnp.dot(sector_cycle, ladder_all, preferred_element_type=F32)
    return (ladder + cycle).astype(BF)


def body(*args):
    update, crowded = compact(*args)
    return lax.cond(crowded[0] > 0, lambda: dense(*args), lambda: update)


def solution(mesh):
    in_specs = (P("occ", ("rep", "vir")), P("rep", "vir"), P("occ", None), P(), P())
    return jax.shard_map(body, mesh=mesh, in_specs=in_specs, out_specs=P("occ", "vir"), check_vma=False)
```

```python
import functools

import jax
import jax.numpy as jnp
from jax import lax
from jax.experimental import pallas as pl
from jax.experimental.pallas import tpu as pltpu
from jax.sharding import PartitionSpec as P

MESH = pl.DeviceIdType.MESH
BF, F32 = jnp.bfloat16, jnp.float32
NX, NY, NZ = 4, 8, 12
GROUPS, ROWS, CAP, LANES = 6, 512, 96, 128
OWN, COLS, DEPTH = 96, 384, 3072
HALF = CAP // 2
MAIN, SPARE = 80, LANES - CAP
Y_ORDER = (0, 1, 2, 3, 7, 6, 5, 4)
LAST_Y = Y_ORDER[-1]
Z_STEPS = (1, 2, 3, 9, 10, 11)
TOP = 32000.0


def onehot(labels):
    width = labels.shape[1]
    rows = lax.broadcasted_iota(jnp.int32, (16, width), 0)
    return jnp.where(jnp.broadcast_to(labels, (16, width)) == rows, 1.0, 0.0).astype(BF)


def meet(a, b):
    return lax.dot_general(a, b, (((0,), (0,)), ((), ())), preferred_element_type=F32)


def kernel(
    amps_in, lad_ref, cyc_ref, occ_in, vir_in, out_ref, flag_ref,
    amps_ref, occ_ref, vir_ref, lad, cyc, cbuf, racc, rin, pbuf, psc, qbuf, sbuf, ucat, lcat, omask,
    load_sem, y_send, x_send, c_recv, r_send, r_recv, q_send, s_send, q_recv, s_recv,
    g_send, gs_send, g_recv, gs_recv, f_send, fs_send, ready_x, ready_y, ready_z, ready_c,
):
    rep, occ, vir = lax.axis_index("rep"), lax.axis_index("occ"), lax.axis_index("vir")
    x, y, z, core = vir // NY, vir % NY, (rep // 2) * GROUPS + occ, rep % 2

    def at(x1, y1, z1, core1):
        return {"rep": (z1 // GROUPS) * 2 + core1, "occ": z1 % GROUPS, "vir": x1 * NY + y1}

    def turn_x(x1):
        return jnp.where(x1 < 2, x1, 5 - x1)

    def turn_y(y1):
        return jnp.where(y1 < 4, y1, 11 - y1)

    def copy(src, dst, send, recv, where):
        return pltpu.make_async_remote_copy(
            src_ref=src, dst_ref=dst, send_sem=send, recv_sem=recv, device_id=where, device_id_type=MESH
        )

    loads = [
        pltpu.make_async_copy(a, b, load_sem.at[i])
        for i, (a, b) in enumerate(((occ_in, occ_ref), (vir_in, vir_ref), (amps_in, amps_ref)), 2)
    ]
    for load in loads:
        load.start()
    load_lad = pltpu.make_async_copy(lad_ref, lad, load_sem.at[0])
    load_cyc = pltpu.make_async_copy(cyc_ref, cyc, load_sem.at[1])
    load_lad.start()
    load_cyc.start()

    contacts = [((x, y1, z, core), ready_y.at[y], turn_y(y1) > turn_y(y), y1 != y) for y1 in range(NY)]
    contacts += [((x1, y, z, core), ready_x.at[x], turn_x(x1) > turn_x(x), x1 != x) for x1 in range(NX)]
    contacts += [
        ((x, y, (z + d) % NZ, core), ready_z.at[NZ - d], (z + d) % NZ > z, core < 2) for d in Z_STEPS
    ]
    contacts += [((x, y, z, 1 - core), ready_c, core == 0, core < 2)]
    barrier = pltpu.get_barrier_semaphore()
    sibling = at(x, y, z, 1 - core)
    for where, _, later, other in contacts:
        @pl.when(later & other)
        def _(where=where):
            pl.semaphore_signal(barrier, inc=1, device_id=at(*where), device_id_type=MESH)

    lower = sum(((z + d) % NZ < z).astype(jnp.int32) for d in Z_STEPS)
    before = turn_x(x) + turn_y(y) + lower + core

    @pl.when(before > 0)
    def _():
        pl.semaphore_wait(barrier, before)
    for where, ready, later, other in contacts:
        @pl.when(jnp.logical_not(later) & other)
        def _(where=where, ready=ready):
            pl.semaphore_signal(ready, inc=1, device_id=at(*where), device_id_type=MESH)

    for load in loads:
        load.wait()

    upper = lax.broadcasted_iota(jnp.int32, (ROWS, ROWS), 0) < lax.broadcasted_iota(jnp.int32, (ROWS, ROWS), 1)
    upper = jnp.where(upper, 1.0, 0.0).astype(BF)
    slot_ids = lax.broadcasted_iota(jnp.int32, (LANES, ROWS), 0).astype(F32)

    def slot_matrix(hot):
        before = jnp.dot(hot, upper, preferred_element_type=F32)
        rank = jnp.sum(before * hot.astype(F32), axis=0, keepdims=True)
        return jnp.where(jnp.broadcast_to(rank, (LANES, ROWS)) == slot_ids, 1.0, 0.0)

    occ_hot = onehot(occ_ref[:, pl.ds(pl.multiple_of(occ * ROWS, ROWS), ROWS)])
    own_slots = slot_matrix(occ_hot)
    first = (rep * 32 + vir) * OWN
    base = pl.multiple_of(jnp.minimum(first // 128, 94) * 128, 128)
    window = jnp.broadcast_to(vir_ref[:, pl.ds(base, 256)], (8, 256))
    window = pltpu.roll(window, (256 - (first - base)) % 256, 1)
    own_hot = onehot(window[0:1, :128])
    mask = meet(own_hot, occ_hot)[:OWN, :]
    sector = jnp.where(mask > 0.5, amps_ref[...].astype(F32), 0.0).astype(BF)

    def place(columns, slots):
        return lax.dot_general(
            columns, slots.astype(BF), (((1,), (1,)), ((), ())), preferred_element_type=F32
        )

    no_slots = jnp.zeros((SPARE, ROWS), F32)
    chunk = place(sector[:MAIN], jnp.concatenate([own_slots[:CAP], no_slots], axis=0))
    aside = [
        place(sector[MAIN:], jnp.concatenate([no_slots] * 3 + [own_slots[j * SPARE:(j + 1) * SPARE]], axis=0))
        for j in range(3)
    ]
    aside.append(jnp.zeros((MAIN - 3 * (OWN - MAIN), LANES), F32))
    cbuf[vir] = (chunk + jnp.concatenate(aside, axis=0)).astype(BF)

    def y_copy(y1):
        return copy(cbuf.at[vir], cbuf.at[vir], y_send.at[y1], c_recv.at[vir], at(x, y1, z, core))

    def x_copy(y1, d):
        v = x * NY + y1
        return copy(cbuf.at[v], cbuf.at[v], x_send.at[y1, d], c_recv.at[v], at((x + d) % NX, y, z, core))

    def c_wait(v):
        copy(cbuf.at[v], cbuf.at[v], y_send.at[0], c_recv.at[v], at(x, (y + 1) % NY, z, core)).wait_recv()

    def relay(y1):
        for d in (2, 1, 3):
            x_copy(y1, d).start()

    for y1 in Y_ORDER:
        @pl.when(turn_y(y1) < turn_y(y))
        def _(y1=y1):
            y_copy(y1).start()
    for x1 in range(NX):
        @pl.when(turn_x(x1) > turn_x(x))
        def _(x1=x1):
            pl.semaphore_wait(ready_x.at[x1], 1)
    relay(y)

    col_hot = onehot(vir_ref[:, pl.ds(pl.multiple_of(vir * COLS, 128), COLS)])

    def mask_ladder(i):
        blocks = slice(4 * i, 4 * i + 4)
        row_hot = onehot(vir_ref[:, pl.ds(pl.multiple_of(rep * DEPTH + i * COLS, 128), COLS)])
        keep = meet(row_hot, col_hot)
        rows = lad[blocks].reshape(COLS, COLS).astype(F32)
        lad[blocks] = jnp.where(keep > 0.5, rows, 0.0).astype(BF).reshape(4, OWN, COLS)

    def pack_cycle(g):
        hot = onehot(occ_ref[:, g * ROWS:(g + 1) * ROWS])
        most = jnp.max(jnp.sum(hot.astype(F32), axis=1, keepdims=True))
        group_slots = slot_matrix(hot).astype(BF)
        keep = meet(occ_hot, hot)
        part = jnp.where(keep > 0.5, cyc[:, g * ROWS:(g + 1) * ROWS].astype(F32), 0.0).astype(BF)
        moved = lax.dot_general(part, group_slots, (((1,), (1,)), ((), ())), preferred_element_type=F32)
        ucat[:, g * LANES:(g + 1) * LANES] = moved.astype(BF)
        return most

    def prepare():
        load_lad.wait()
        for i in range(8):
            mask_ladder(i)
        load_cyc.wait()
        worst = jnp.zeros((), F32)
        for g in range(GROUPS):
            worst = jnp.maximum(worst, pack_cycle(g))
        flag_ref[0] = jnp.where(worst > CAP, 1, 0)
        plain = own_slots.T.astype(BF)
        ucat[:, 6 * LANES:7 * LANES] = plain
        ucat[:, 7 * LANES:8 * LANES] = plain
        omask[...] = meet(occ_hot, col_hot)
        lcat[...] = jnp.zeros_like(lcat)

    early = turn_y(y) < 3
    pl.when(early)(prepare)
    for y1 in Y_ORDER:
        @pl.when(turn_y(y1) > turn_y(y))
        def _(y1=y1):
            pl.semaphore_wait(ready_y.at[y1], 1)
            y_copy(y1).start()
    for d in (1, 7, 2, 6, 3, 5, 4):
        source = lax.rem(y + d, NY)

        @pl.when(source != LAST_Y)
        def _(source=source):
            c_wait(x * NY + source)
            relay(source)

    @pl.when(y != LAST_Y)
    def _():
        c_wait(x * NY + LAST_Y)
        relay(LAST_Y)
    pl.when(jnp.logical_not(early))(prepare)

    def product(start):
        block, rows = cbuf[pl.ds(start, NY)], lad[pl.ds(start, NY)]

        def dot(a, b):
            a, b = a.reshape(-1, LANES), b.reshape(-1, COLS)
            return lax.dot_general(a, b, (((0,), (0,)), ((), ())), preferred_element_type=F32)

        main = dot(block[:, :MAIN], rows[:, :MAIN])[:CAP]
        step = OWN - MAIN
        aside = [dot(block[:, j * step:(j + 1) * step], rows[:, MAIN:])[CAP:] for j in range(3)]
        return main + jnp.concatenate(aside, axis=0)

    racc[...] = product(x * NY)
    for d in (1, 3, 2):
        start = lax.rem(x + d, NX) * NY
        for y1 in range(NY):
            c_wait(start + y1)
        racc[...] += product(start)

    mine = pl.ds(pl.multiple_of(core * HALF, HALF), HALF)
    theirs = pl.ds(pl.multiple_of((1 - core) * HALF, HALF), HALF)
    half_copy = copy(racc.at[theirs], rin, r_send, r_recv, sibling)

    @pl.when(core == 0)
    def _():
        pl.semaphore_wait(ready_c, 1)
    half_copy.start()
    half_copy.wait_recv()
    total = racc[mine, :] + rin[...]

    def pack(values, into, scale):
        largest = jnp.max(jnp.max(jnp.abs(values), axis=1, keepdims=True), axis=0, keepdims=True)
        largest = jnp.maximum(largest, 1e-30)
        into[...] = jnp.round(values * (TOP / largest)).astype(jnp.int32).astype(jnp.int16)
        scale[...] = jnp.broadcast_to(largest * (1.0 / TOP), (8, 128))

    def unpack(packed, scale):
        return packed[...].astype(jnp.int32).astype(F32) * scale[0:1, 0:1]

    def send(q, s, to_q, to_s, sems, where):
        return copy(q, to_q, sems[0], sems[1], where), copy(s, to_s, sems[2], sems[3], where)

    def part_copy(i):
        d = (3, 9)[i]
        sems = q_send.at[i], q_recv.at[i], s_send.at[i], s_recv.at[i]
        return send(pbuf.at[2], psc.at[2], pbuf.at[i], psc.at[i], sems, at(x, y, (z + d) % NZ, core))

    group = lax.rem(z + 3, GROUPS)

    def group_copy(d):
        sems = g_send.at[d % NZ], g_recv.at[group, core], gs_send.at[d % NZ], gs_recv.at[group, core]
        to = qbuf.at[group, mine], sbuf.at[group, core]
        return send(*to, *to, sems, at(x, y, (z + d + NZ) % NZ, core))

    def side_copy(g):
        sems = f_send.at[g], g_recv.at[g, core], fs_send.at[g], gs_recv.at[g, core]
        to = qbuf.at[g, mine], sbuf.at[g, core]
        return send(*to, *to, sems, sibling)

    def group_wait(g, half):
        rows = pl.ds(pl.multiple_of(half * HALF, HALF), HALF)
        to = qbuf.at[g, rows], sbuf.at[g, half]
        sems = f_send.at[0], g_recv.at[g, half], fs_send.at[0], gs_recv.at[g, half]
        for c in send(*to, *to, sems, sibling):
            c.wait_recv()

    pack(total, pbuf.at[2], psc.at[2])
    for d in Z_STEPS:
        @pl.when((z + d) % NZ > z)
        def _(d=d):
            pl.semaphore_wait(ready_z.at[d], 1)
    for i in range(2):
        for c in part_copy(i):
            c.start()
    for i in range(2):
        for c in part_copy(i):
            c.wait_recv()
    both = unpack(pbuf.at[0], psc.at[0]) + unpack(pbuf.at[1], psc.at[1])
    pack(both, qbuf.at[group, mine], sbuf.at[group, core])
    far = jnp.where(core == 0, 3, 9)
    far_copy = [
        copy(a, a, sems[0], sems[1], at(x, y, lax.rem(z + far, NZ), core))
        for a, sems in (
            (qbuf.at[group, mine], (g_send.at[3], g_recv.at[group, core])),
            (sbuf.at[group, core], (gs_send.at[3], gs_recv.at[group, core])),
        )
    ]
    for c in far_copy:
        c.start()
    for d in (2, -2, 1, -1):
        for c in group_copy(d):
            c.start()
    for c in side_copy(group):
        c.start()
    for d in (1, -1, 2, -2, 3):
        g = lax.rem(z - d + 3 + NZ, GROUPS)
        group_wait(g, core)
        for c in side_copy(g):
            c.start()

    def whole(g):
        scale = jnp.concatenate(
            [jnp.broadcast_to(sbuf[g, h][0:1, 0:1], (HALF, COLS)) for h in range(2)], axis=0
        )
        return qbuf[g].astype(jnp.int32).astype(F32) * scale

    for g in range(GROUPS):
        group_wait(g, 1 - core)
        lcat[g * LANES:g * LANES + CAP, :] = whole(g).astype(BF)
    own = whole(occ)
    high = own.astype(BF)
    lcat[6 * LANES:6 * LANES + CAP, :] = high
    lcat[7 * LANES:7 * LANES + CAP, :] = (own - high.astype(F32)).astype(BF)
    result = jnp.dot(ucat[...], lcat[...], preferred_element_type=F32)
    out_ref[...] = jnp.where(omask[...] > 0.5, result, 0.0).astype(BF)

    for y1 in range(NY):
        @pl.when(y1 != y)
        def _(y1=y1):
            y_copy(y1).wait_send()
        for d in range(1, NX):
            x_copy(y1, d).wait_send()
    half_copy.wait_send()
    for i in range(2):
        for c in part_copy(i):
            c.wait_send()
    for c in far_copy:
        c.wait_send()
    for d in (2, -2, 1, -1):
        for c in group_copy(d):
            c.wait_send()
    for g in range(GROUPS):
        for c in side_copy(g):
            c.wait_send()


def compact(amplitudes, ladder_ints, cycle_ints, occ_irrep, vir_irrep):
    vmem, dma = pltpu.VMEM, pltpu.SemaphoreType.DMA
    return pl.pallas_call(
        kernel,
        out_shape=(jax.ShapeDtypeStruct((ROWS, COLS), BF), jax.ShapeDtypeStruct((1,), jnp.int32)),
        in_specs=[pl.BlockSpec(memory_space=pl.ANY)] * 5,
        out_specs=(pl.BlockSpec(memory_space=vmem), pl.BlockSpec(memory_space=pltpu.SMEM)),
        scratch_shapes=[
            vmem((OWN, ROWS), BF),
            vmem((1, GROUPS * ROWS), jnp.int32),
            vmem((1, NX * NY * COLS), jnp.int32),
            vmem((NX * NY, OWN, COLS), BF),
            vmem((ROWS, GROUPS * ROWS), BF),
            vmem((NX * NY, MAIN, LANES), BF),
            vmem((CAP, COLS), F32),
            vmem((HALF, COLS), F32),
            vmem((3, HALF, COLS), jnp.int16),
            vmem((3, 8, 128), F32),
            vmem((GROUPS, CAP, COLS), jnp.int16),
            vmem((GROUPS, 2, 8, 128), F32),
            vmem((ROWS, 8 * LANES), BF),
            vmem((8 * LANES, COLS), BF),
            vmem((ROWS, COLS), F32),
            dma((5,)),
            dma((NY,)),
            dma((NY, NX)),
            dma((NX * NY,)),
            dma,
            dma,
            dma((2,)),
            dma((2,)),
            dma((2,)),
            dma((2,)),
            dma((NZ,)),
            dma((NZ,)),
            dma((GROUPS, 2)),
            dma((GROUPS, 2)),
            dma((GROUPS,)),
            dma((GROUPS,)),
            pltpu.SemaphoreType.REGULAR((NX,)),
            pltpu.SemaphoreType.REGULAR((NY,)),
            pltpu.SemaphoreType.REGULAR((NZ,)),
            pltpu.SemaphoreType.REGULAR,
        ],
        compiler_params=pltpu.CompilerParams(
            collective_id=0, has_side_effects=True, vmem_limit_bytes=48 * 1024 * 1024
        ),
        cost_estimate=pl.CostEstimate(flops=2_000_000_000, bytes_accessed=6_500_000, transcendentals=0),
    )(amplitudes.T, ladder_ints.reshape(NX * NY, OWN, COLS), cycle_ints, occ_irrep.reshape(1, -1), vir_irrep.reshape(1, -1))


def ring(axis, block, n):
    me = lax.axis_index(axis)
    perm = [(i, (i + 1) % n) for i in range(n)]
    held = jnp.zeros((n,) + block.shape, block.dtype)

    def step(s, carry):
        held, block = carry
        held = lax.dynamic_update_index_in_dim(held, block, (me - s + n) % n, 0)
        return held, lax.ppermute(block, axis, perm)

    held, _ = lax.fori_loop(0, n, step, (held, block))
    return held


def dense(amplitudes, ladder_ints, cycle_ints, occ_irrep, vir_irrep):
    rep_pos, vir_pos, occ_pos = lax.axis_index("rep"), lax.axis_index("vir"), lax.axis_index("occ")
    zero = jnp.zeros((), BF)
    occ_own = lax.dynamic_slice_in_dim(occ_irrep, occ_pos * ROWS, ROWS)
    own_labels = lax.dynamic_slice_in_dim(vir_irrep, (rep_pos * 32 + vir_pos) * OWN, OWN)
    sector_amps = jnp.where(occ_own[:, None] == own_labels[None, :], amplitudes, zero)
    group_labels = lax.dynamic_slice_in_dim(vir_irrep, rep_pos * DEPTH, DEPTH)
    column_labels = lax.dynamic_slice_in_dim(vir_irrep, vir_pos * COLS, COLS)
    sector_ladder = jnp.where(group_labels[:, None] == column_labels[None, :], ladder_ints, zero)
    sector_cycle = jnp.where(occ_own[:, None] == occ_irrep[None, :], cycle_ints, zero)
    gathered = ring("vir", sector_amps, NX * NY).transpose(1, 0, 2).reshape(ROWS, DEPTH)
    partial_ladder = jnp.dot(gathered, sector_ladder, preferred_element_type=F32)
    parts = ring("rep", partial_ladder, 4)
    ladder = (parts[0] + parts[1]) + (parts[2] + parts[3])
    ladder_all = ring("occ", ladder.astype(BF), GROUPS).reshape(GROUPS * ROWS, COLS)
    cycle = jnp.dot(sector_cycle, ladder_all, preferred_element_type=F32)
    return (ladder + cycle).astype(BF)


def body(*args):
    update, crowded = compact(*args)
    return lax.cond(crowded[0] > 0, lambda: dense(*args), lambda: update)


def solution(mesh):
    in_specs = (P("occ", ("rep", "vir")), P("rep", "vir"), P("occ", None), P(), P())
    return jax.shard_map(body, mesh=mesh, in_specs=in_specs, out_specs=P("occ", "vir"), check_vma=False)
```
